256 devices in a mesh: band: 4 (over x), tile: 64 (over y, z, core).
Axes of the slice: x: 4, y: 4, z: 8, core: 2. Of those that a mesh axis runs over, the one named last changes fastest.
Arguments:
- series: float32 [1048576], P('tile'), may hold values from -6 to 6
- block_pick: int32 [4, 64, 64], P('band', 'tile'), may hold values from 0 to 7
- tile_pairs: int32 [4, 64, 2, 8], P('band', 'tile'), may hold values from 0 to 63
- tile_counts: int32 [4, 64], P('band', 'tile'), may hold values from 1 to 8, as said below
Outputs:
- profile: float32 [1048576], P('tile')
The draws below stay inside these ranges and needn't reach their ends.
Inputs may be any that keep to these rules, and one draw needn't show every extreme that they name: Each device lists tiles only in its first tile_counts slots; some device uses all 8 slots.
All inputs are finite; a program needn't handle non-finite values.
Results may differ from the reference program's by a relative error of at most 0.0003.
Values sent between devices are 32-bit elements; how exact they have to be, the bound alone decides.
No kernel may reach another device: no remote copies, remote signals or barrier semaphores. Data moves between devices by JAX's collectives and lax.ppermute only.
A program may use at most 64 MiB of HBM per device.

```python
import jax
import jax.numpy as jnp
from jax import lax

SUBLEN = 64
BLOCK = 2048
BLK_DEV = 8
SLOTS = 8
EXCL = 16
BANDS = 4
OWNERS = 64
BLOCKS = 512
SAMPLES = 1048576


def draw_tile_pairs(key, part):
    key = jax.random.fold_in(key, 11)
    key_first, key_second, key_same = jax.random.split(key, 3)
    first = jax.random.randint(key_first, (BANDS, OWNERS, SLOTS), 0, OWNERS)
    second = jax.random.randint(key_second, (BANDS, OWNERS, SLOTS), 0, OWNERS)
    same = jax.random.randint(key_same, (BANDS, OWNERS, SLOTS), 0, 8) == 0
    second = jnp.where(same, first, second)
    return jnp.stack([first, second], axis=2).astype(jnp.int32)


def draw_tile_counts(key, part):
    key = jax.random.fold_in(key, 23)
    key_level, key_busy = jax.random.split(key)
    level = jax.random.randint(key_level, (BANDS * OWNERS,), 0, SLOTS)
    counts = 1 + level * level // SLOTS
    busiest = jax.random.randint(key_busy, (), 0, BANDS * OWNERS)
    counts = jnp.where(jnp.arange(BANDS * OWNERS) == busiest, SLOTS, counts)
    return counts.reshape(BANDS, OWNERS).astype(jnp.int32)


def with_ends(array, key, low, largest):
    place = [jax.random.randint(jax.random.fold_in(key, axis), (), 0, length) for axis, length in enumerate(array.shape)]
    longest = array.shape.index(max(array.shape))
    neighbour = place[:longest] + [(place[longest] + 1) % array.shape[longest]] + place[longest + 1:]
    return array.at[tuple(place)].set(low).at[tuple(neighbour)].set(largest)


def block_scale(key, extent, pieces, least, top_value):
    loudness = 1.0
    for position, parts in pieces:
        heights = jax.random.uniform(jax.random.fold_in(jax.random.fold_in(key, 6), position), (parts,), jnp.float32, least / len(pieces), top_value / len(pieces))
        loudness = loudness * jnp.repeat(jnp.exp(heights), extent[position] // parts).reshape((-1,) + (1,) * (len(extent) - 1 - position))
    return loudness


def gaussian(key, extent, deviation, limit, shards=(), held_as=jnp.bfloat16):
    result = deviation * jax.random.normal(key, extent, jnp.float32)
    if shards:
        result = result * block_scale(key, extent, shards, -0.22, 0.18)
    return jnp.clip(result, -limit, limit).astype(held_as)


def setup_inputs(seed: int = 0) -> dict:
    streams_of = jax.random.split(jax.random.key(seed), 5)
    return {
        "series": gaussian(streams_of[0], (SAMPLES,), 1.0, 6.0, ((0, 64),), jnp.float32),
        "block_pick": with_ends(jax.random.randint(streams_of[1], (BANDS, OWNERS, OWNERS), 0, BLK_DEV), jax.random.fold_in(streams_of[1], 1), 0, BLK_DEV - 1).astype(jnp.int32),
        "tile_pairs": draw_tile_pairs(jax.random.fold_in(streams_of[4], 71), 0),
        "tile_counts": draw_tile_counts(jax.random.fold_in(streams_of[4], 71), 0),
    }


def build_windows(extended, length):
    last = extended.ndim - 1
    stacked = jnp.stack([lax.slice_in_dim(extended, offset, offset + length, axis=last) for offset in range(SUBLEN)], axis=-2)
    center = lax.optimization_barrier(jnp.mean(stacked, axis=-2, keepdims=True))
    shifted = stacked - center
    spread = lax.optimization_barrier(jnp.mean(shifted * shifted, axis=-2, keepdims=True))
    return shifted * lax.rsqrt(spread + 1e-05)

def tile_minima(rows_win, cols_win, row_start, col_start):
    products = jnp.einsum('ki,kj->ij', rows_win, cols_win, precision=lax.Precision.HIGHEST, preferred_element_type=jnp.float32)
    distance = 2.0 - products * (2.0 / SUBLEN)
    positions = jnp.arange(BLOCK, dtype=jnp.int32)
    row_pos = row_start + positions
    col_pos = col_start + positions
    gap = row_pos[:, None] - col_pos[None, :]
    distance = jnp.where(jnp.abs(gap) < EXCL, 4.0, distance)
    return (lax.optimization_barrier(jnp.min(distance, axis=1)), lax.optimization_barrier(jnp.min(distance, axis=0)))

def reference(series, block_pick, tile_pairs, tile_counts):
    extended = jnp.concatenate([series, jnp.zeros((SUBLEN,), jnp.float32)])
    windows = build_windows(extended, SAMPLES)
    groups = tile_counts.shape[0]
    owners = tile_counts.shape[1]

    def visit(profile, flat):
        band_id = flat // (owners * SLOTS)
        owner_id = flat // SLOTS % owners
        slot_id = flat % SLOTS
        first = tile_pairs[band_id, owner_id, 0, slot_id]
        second = tile_pairs[band_id, owner_id, 1, slot_id]
        block_a = (first * BLK_DEV + block_pick[band_id, first, owner_id]).astype(jnp.int32)
        block_b = (second * BLK_DEV + block_pick[band_id, second, owner_id]).astype(jnp.int32)
        valid = slot_id < tile_counts[band_id, owner_id]

        def compute():
            rows_win = lax.dynamic_slice_in_dim(windows, (block_a * BLOCK).astype(jnp.int32), BLOCK, 1)
            cols_win = lax.dynamic_slice_in_dim(windows, (block_b * BLOCK).astype(jnp.int32), BLOCK, 1)
            return tile_minima(rows_win, cols_win, block_a * BLOCK, block_b * BLOCK)

        def skipped():
            filler = jnp.full((BLOCK,), 4.0, windows.dtype)
            return (filler, filler)
        row_min, col_min = lax.cond(valid, compute, skipped)
        profile = profile.at[block_a].min(row_min)
        profile = profile.at[block_b].min(col_min)
        return (profile, None)
    start = jnp.full((BLOCKS, BLOCK), 4.0, jnp.float32)
    profile, unused = lax.scan(visit, start, jnp.arange(groups * owners * SLOTS, dtype=jnp.int32))
    return profile.reshape(SAMPLES)
```

```python
import functools

import jax
import jax.numpy as jnp
from jax import lax
from jax.experimental import pallas as pl
from jax.experimental.pallas import tpu as pltpu
from jax.sharding import PartitionSpec as P

SUBLEN = 64
BLOCK = 2048
BLK_DEV = 8
EXCL = 16
LANES = 128
ROW = BLOCK + LANES
CHUNK = 256


def pick_rows(series, picks, myself):
    bodies = series.reshape(BLK_DEV, BLOCK)
    tails = jnp.concatenate([bodies[1:, :SUBLEN], jnp.zeros((1, SUBLEN), jnp.float32)])
    head = jnp.broadcast_to(series[: SUBLEN - 1], (BLK_DEV, SUBLEN - 1))
    numbers = (myself * BLK_DEV + jnp.arange(BLK_DEV)).astype(jnp.float32)[:, None]
    rows = jnp.concatenate([bodies, tails, head, numbers], axis=1)
    return rows[picks][:, None, :]


def whole_row(recv_ref, owner, owners):
    row = recv_ref[owner]
    extra = row[:, BLOCK:]
    lane = lax.broadcasted_iota(jnp.int32, (1, LANES), 1)
    number = jnp.sum(jnp.where(lane == LANES - 1, extra, 0.0)).astype(jnp.int32)
    following = recv_ref[jnp.minimum(owner + 1, owners - 1)][:, BLOCK:]
    following = pltpu.roll(following, SUBLEN, 1)
    following = jnp.where(owner == owners - 1, 0.0, following)
    extra = jnp.where(lax.rem(number, BLK_DEV) == BLK_DEV - 1, following, extra)
    return jnp.concatenate([row[:, :BLOCK], extra], axis=1), number


def windows(row):
    wide = jnp.broadcast_to(row, (8, ROW))
    sub = lax.broadcasted_iota(jnp.int32, (8, ROW), 0)
    for bit in (1, 2, 4):
        wide = jnp.where((sub & bit) != 0, pltpu.roll(wide, ROW - bit, 1), wide)
    parts = [wide[:, :BLOCK]]
    for a in range(1, SUBLEN // 8):
        parts.append(pltpu.roll(wide, ROW - 8 * a, 1)[:, :BLOCK])
    mean = jnp.sum(functools.reduce(jnp.add, parts), axis=0, keepdims=True) * (1.0 / SUBLEN)
    parts = [part - mean for part in parts]
    squares = functools.reduce(jnp.add, [part * part for part in parts])
    spread = jnp.sum(squares, axis=0, keepdims=True) * (1.0 / SUBLEN)
    inverse = lax.rsqrt(spread + 1e-05)
    znorm = jnp.concatenate([part * inverse for part in parts], axis=0)
    high = znorm.astype(jnp.bfloat16)
    low = (znorm - high.astype(jnp.float32)).astype(jnp.bfloat16)
    return high, low


def tiles_kernel(count_ref, pairs_ref, recv_ref, out_ref, lhs, rhs, row_acc, col_acc):
    owners = recv_ref.shape[0]
    out_ref[...] = jnp.full(out_ref.shape, 4.0, jnp.float32)

    def columns(n):
        return pl.ds(pl.multiple_of(n * CHUNK, CHUNK), CHUNK)

    def slot(s, carry):
        first = pairs_ref[0, s]
        second = pairs_ref[1, s]
        cols, col_number = whole_row(recv_ref, second, owners)
        high, low = windows(cols)
        rhs[0:64] = high
        rhs[64:128] = high
        rhs[128:192] = low
        rhs[192:256] = low
        rows, row_number = whole_row(recv_ref, first, owners)
        high, low = windows(rows)
        both = jnp.concatenate([high, low], axis=0)
        for q in range(BLOCK // LANES):
            part = both[:, q * LANES : (q + 1) * LANES].astype(jnp.float32).T.astype(jnp.bfloat16)
            lhs[q * LANES : (q + 1) * LANES, 0:128] = part
            lhs[q * LANES : (q + 1) * LANES, 128:256] = part
        row_acc[...] = jnp.full(row_acc.shape, -1.0 * SUBLEN, jnp.float32)
        ahead = (row_number - col_number) * BLOCK
        near = jnp.abs(ahead) <= BLOCK

        def sweep(masked):
            def one_chunk(n, carry):
                weights = rhs[:, columns(n)]
                best = jnp.full((8, CHUNK), -1.0 * SUBLEN, jnp.float32)
                for m in range(BLOCK // CHUNK):
                    here = slice(m * CHUNK, (m + 1) * CHUNK)
                    products = jnp.dot(lhs[here], weights, preferred_element_type=jnp.float32)
                    if masked:
                        gap = (
                            (ahead + m * CHUNK - n * CHUNK)
                            + lax.broadcasted_iota(jnp.int32, (CHUNK, CHUNK), 0)
                            - lax.broadcasted_iota(jnp.int32, (CHUNK, CHUNK), 1)
                        )
                        products = jnp.where(jnp.abs(gap) < EXCL, -1.0 * SUBLEN, products)
                    best = jnp.maximum(best, jnp.max(products.reshape(CHUNK // 8, 8, CHUNK), axis=0))
                    row_acc[here] = jnp.maximum(
                        row_acc[here], jnp.maximum(products[:, :LANES], products[:, LANES:])
                    )
                col_acc[:, columns(n)] = best
                return carry

            lax.fori_loop(0, BLOCK // CHUNK, one_chunk, 0)

        @pl.when(jnp.logical_not(near))
        def _():
            sweep(False)

        @pl.when(near)
        def _():
            sweep(True)

        row_parts = [
            jnp.max(row_acc[q * LANES : (q + 1) * LANES].T, axis=0, keepdims=True)
            for q in range(BLOCK // LANES)
        ]
        for q in range(BLOCK // LANES):
            least = 2.0 - row_parts[q] * (2.0 / SUBLEN)
            out_ref[first, q : q + 1] = jnp.minimum(out_ref[first, q : q + 1], least)
        col_best = 2.0 - jnp.max(col_acc[...], axis=0, keepdims=True) * (2.0 / SUBLEN)
        for q in range(BLOCK // LANES):
            least = col_best[:, q * LANES : (q + 1) * LANES]
            out_ref[second, q : q + 1] = jnp.minimum(out_ref[second, q : q + 1], least)
        return carry

    lax.fori_loop(0, count_ref[0, 0], slot, 0)


def tiles(count, pairs, received):
    owners = received.shape[0]
    return pl.pallas_call(
        tiles_kernel,
        out_shape=jax.ShapeDtypeStruct((owners, BLOCK // LANES, LANES), jnp.float32),
        in_specs=[
            pl.BlockSpec(memory_space=pltpu.SMEM),
            pl.BlockSpec(memory_space=pltpu.SMEM),
            pl.BlockSpec(memory_space=pltpu.VMEM),
        ],
        out_specs=pl.BlockSpec(memory_space=pltpu.VMEM),
        scratch_shapes=[
            pltpu.VMEM((BLOCK, 256), jnp.bfloat16),
            pltpu.VMEM((256, BLOCK), jnp.bfloat16),
            pltpu.VMEM((BLOCK, LANES), jnp.float32),
            pltpu.VMEM((8, BLOCK), jnp.float32),
        ],
        compiler_params=pltpu.CompilerParams(vmem_limit_bytes=40 * 1024 * 1024),
    )(count, pairs, received)


def owned_kernel(picks_ref, returned_ref, out_ref):
    out_ref[...] = jnp.full(out_ref.shape, 4.0, jnp.float32)
    for t in range(returned_ref.shape[0]):
        which = picks_ref[t]
        out_ref[which] = jnp.minimum(out_ref[which], returned_ref[t])


def owned(picks, returned):
    return pl.pallas_call(
        owned_kernel,
        out_shape=jax.ShapeDtypeStruct((BLK_DEV,) + returned.shape[1:], jnp.float32),
        in_specs=[
            pl.BlockSpec(memory_space=pltpu.SMEM),
            pl.BlockSpec(memory_space=pltpu.VMEM),
        ],
        out_specs=pl.BlockSpec(memory_space=pltpu.VMEM),
    )(picks, returned)


def local(series, block_pick, tile_pairs, tile_counts):
    picks = block_pick[0, 0]
    rows = pick_rows(series, picks, lax.axis_index("tile"))
    received = lax.all_to_all(rows, "tile", split_axis=0, concat_axis=0, tiled=True)
    partial_value = tiles(tile_counts, tile_pairs[0, 0], received)
    returned = lax.all_to_all(partial_value, "tile", split_axis=0, concat_axis=0, tiled=True)
    mine = owned(picks, returned)
    bands = lax.axis_size("band")
    others = [
        lax.ppermute(mine, "band", [(i, (i + step) % bands) for i in range(bands)])
        for step in range(1, bands)
    ]
    return functools.reduce(jnp.minimum, others, mine).reshape(BLK_DEV * BLOCK)


def solution(mesh):
    in_specs = (
        P("tile"),
        P("band", "tile", None),
        P("band", "tile", None, None),
        P("band", "tile"),
    )
    out_specs = P("tile")
    return jax.shard_map(local, mesh=mesh, in_specs=in_specs, out_specs=out_specs, check_vma=False)
```

```python
import functools

import jax
import jax.numpy as jnp
from jax import lax
from jax.experimental import pallas as pl
from jax.experimental.pallas import tpu as pltpu
from jax.sharding import PartitionSpec as P

SUBLEN = 64
BLOCK = 2048
BLK_DEV = 8
EXCL = 16
LANES = 128
ROW = BLOCK + LANES
ROW_TILES = ROW // LANES
CHUNK = 256
LEAST = -1.0 * SUBLEN


def rows_kernel(picks_ref, series_ref, out_ref, extra_ref):
    lane = lax.broadcasted_iota(jnp.int32, (1, LANES), 1)
    body = BLOCK // LANES
    first = lax.axis_index("tile") * BLK_DEV
    head = pltpu.roll(series_ref[0, 0:1], SUBLEN, 1)
    for which in range(BLK_DEV):
        after = series_ref[(which + 1) % BLK_DEV, 0:1]
        extra = jnp.where(lane < SUBLEN, after, head)
        number = (first + which).astype(jnp.float32)
        extra_ref[which : which + 1] = jnp.where(lane == LANES - 1, number, extra)
    for t in range(picks_ref.shape[0]):
        which = picks_ref[t]
        out_ref[t * ROW_TILES : t * ROW_TILES + body] = series_ref[which]
        out_ref[t * ROW_TILES + body : (t + 1) * ROW_TILES] = extra_ref[pl.ds(which, 1)]


def rows_to_send(picks, series):
    owners = picks.shape[0]
    rows = pl.pallas_call(
        rows_kernel,
        out_shape=jax.ShapeDtypeStruct((owners * ROW_TILES, LANES), jnp.float32),
        in_specs=[
            pl.BlockSpec(memory_space=pltpu.SMEM),
            pl.BlockSpec(memory_space=pltpu.VMEM),
        ],
        out_specs=pl.BlockSpec(memory_space=pltpu.VMEM),
        scratch_shapes=[pltpu.VMEM((BLK_DEV, LANES), jnp.float32)],
    )(picks, series.reshape(BLK_DEV, BLOCK // LANES, LANES))
    return rows.reshape(owners, 1, ROW)


def stage_row(recv_ref, owner, wide_ref):
    last = recv_ref.shape[0] - 1
    row = recv_ref[owner]
    extra = row[:, BLOCK:]
    number = jnp.broadcast_to(extra[:, LANES - 1 :], (1, LANES)).astype(jnp.int32)
    following = recv_ref[jnp.minimum(owner + 1, last)][:, BLOCK:]
    following = pltpu.roll(following, SUBLEN, 1)
    following = jnp.where(owner == last, 0.0, following)
    extra = jnp.where((number & (BLK_DEV - 1)) == BLK_DEV - 1, following, extra)
    wide = jnp.broadcast_to(jnp.concatenate([row[:, :BLOCK], extra], axis=1), (8, ROW))
    sub = lax.broadcasted_iota(jnp.int32, (8, ROW), 0)
    for bit in (1, 2, 4):
        wide = jnp.where((sub & bit) != 0, pltpu.roll(wide, ROW - bit, 1), wide)
    wide_ref[...] = wide
    return number


def window_chunk(wide_ref, n):
    size = CHUNK + LANES
    wide = wide_ref[:, n * CHUNK : n * CHUNK + size]
    parts = [wide[:, :CHUNK]]
    for a in range(1, SUBLEN // 8):
        parts.append(pltpu.roll(wide, size - 8 * a, 1)[:, :CHUNK])
    mean = jnp.sum(functools.reduce(jnp.add, parts), axis=0, keepdims=True) * (1.0 / SUBLEN)
    parts = [part - mean for part in parts]
    squares = functools.reduce(jnp.add, [part * part for part in parts])
    spread = jnp.sum(squares, axis=0, keepdims=True) * (1.0 / SUBLEN)
    inverse = lax.rsqrt(spread + 1e-05)
    znorm = jnp.concatenate([part * inverse for part in parts], axis=0)
    high = znorm.astype(jnp.bfloat16)
    low = (znorm - high.astype(jnp.float32)).astype(jnp.bfloat16)
    return high, low


def build_chunk(wide_rows, wide_cols, lhs, rhs, n):
    here = slice(n * CHUNK, (n + 1) * CHUNK)
    high, low = window_chunk(wide_cols, n)
    rhs[0:64, here] = high
    rhs[64:128, here] = high
    rhs[128:192, here] = low
    rhs[192:256, here] = low
    high, low = window_chunk(wide_rows, n)
    both = jnp.concatenate([high, low], axis=0).astype(jnp.float32)
    for q in range(CHUNK // LANES):
        part = both[:, q * LANES : (q + 1) * LANES].T.astype(jnp.bfloat16)
        at = slice(n * CHUNK + q * LANES, n * CHUNK + (q + 1) * LANES)
        lhs[at, 0:128] = part
        lhs[at, 128:256] = part


def excluded(products, a, b, ahead_ref):
    def masked(part, first_row, offset, ahead):
        gap = (
            offset + first_row
            + lax.broadcasted_iota(jnp.int32, part.shape, 0)
            - lax.broadcasted_iota(jnp.int32, part.shape, 1)
        )
        hit = jnp.logical_and(jnp.abs(gap) < EXCL, ahead_ref[0:1] == ahead)
        return jnp.where(hit, LEAST, part)

    if a == b:
        return masked(products, 0, 0, 0)
    last = BLOCK // LANES - 1
    if a - b in (1, -last):
        ahead = 0 if a - b == 1 else 1
        return jnp.concatenate([masked(products[:EXCL], 0, LANES, ahead), products[EXCL:]], axis=0)
    if a - b in (-1, last):
        ahead = 0 if a - b == -1 else -1
        top = LANES - EXCL
        return jnp.concatenate([products[:top], masked(products[top:], top, -LANES, ahead)], axis=0)
    return products


def multiply_chunk(lhs, rhs, ahead_ref, row_acc, col_acc, n):
    weights = rhs[:, n * CHUNK : (n + 1) * CHUNK]
    halves = CHUNK // LANES
    best = [None] * halves
    products = jnp.dot(lhs[...], weights, preferred_element_type=jnp.float32)
    for a in range(BLOCK // LANES):
        at = slice(a * LANES, (a + 1) * LANES)
        strip = None
        for v in range(halves):
            b = n * halves + v
            block = excluded(products[at, v * LANES : (v + 1) * LANES], a, b, ahead_ref)
            strip = block if strip is None else jnp.maximum(strip, block)
            top = jnp.max(block.reshape(LANES // 8, 8, LANES), axis=0)
            best[v] = top if best[v] is None else jnp.maximum(best[v], top)
        row_acc[at] = strip if n == 0 else jnp.maximum(row_acc[at], strip)
    for v in range(halves):
        b = n * halves + v
        col_acc[:, b * LANES : (b + 1) * LANES] = best[v]


def finish_chunk(out_ref, first, second, row_acc, col_acc, n):
    for q in range(n * CHUNK // LANES, (n + 1) * CHUNK // LANES):
        at = slice(q * LANES, (q + 1) * LANES)
        most = jnp.max(row_acc[at].T, axis=0, keepdims=True)
        out_ref[first, q : q + 1] = jnp.minimum(out_ref[first, q : q + 1], 2.0 - most * (2.0 / SUBLEN))
        most = jnp.max(col_acc[:, at], axis=0, keepdims=True)
        out_ref[second, q : q + 1] = jnp.minimum(out_ref[second, q : q + 1], 2.0 - most * (2.0 / SUBLEN))


def tiles_kernel(count_ref, pairs_ref, recv_ref, out_ref, wide_rows, wide_cols, *buffers):
    sets = (buffers[:5], buffers[5:])
    count = count_ref[0, 0]
    out_ref[...] = jnp.full(out_ref.shape, 4.0, jnp.float32)
    for lhs, rhs, ahead, row_acc, col_acc in sets[1:]:
        row_acc[...] = jnp.full(row_acc.shape, LEAST, jnp.float32)
        col_acc[...] = jnp.full(col_acc.shape, LEAST, jnp.float32)

    def stage(s, ahead_ref):
        rows = stage_row(recv_ref, pairs_ref[0, s], wide_rows)
        cols = stage_row(recv_ref, pairs_ref[1, s], wide_cols)
        ahead_ref[...] = jnp.broadcast_to(rows - cols, ahead_ref.shape)

    stage(0, sets[0][2])
    for n in range(BLOCK // CHUNK):
        build_chunk(wide_rows, wide_cols, sets[0][0], sets[0][1], n)

    def phase(now, other, s):
        before = jnp.clip(s - 1, 0, count - 1)
        stage(jnp.minimum(s + 1, count - 1), other[2])
        for n in range(BLOCK // CHUNK):
            multiply_chunk(*now, n)
            build_chunk(wide_rows, wide_cols, other[0], other[1], n)
            finish_chunk(out_ref, pairs_ref[0, before], pairs_ref[1, before], other[3], other[4], n)

    def two(i, carry):
        phase(sets[0], sets[1], 2 * i)
        phase(sets[1], sets[0], 2 * i + 1)
        return carry

    steps = (count + 1) // 2
    lax.fori_loop(0, steps, two, 0)
    final = count - 1
    for n in range(BLOCK // CHUNK):
        finish_chunk(out_ref, pairs_ref[0, final], pairs_ref[1, final], sets[1][3], sets[1][4], n)


def tiles(count, pairs, received):
    owners = received.shape[0]
    one = [
        pltpu.VMEM((BLOCK, 256), jnp.bfloat16),
        pltpu.VMEM((256, BLOCK), jnp.bfloat16),
        pltpu.VMEM((8, LANES), jnp.int32),
        pltpu.VMEM((BLOCK, LANES), jnp.float32),
        pltpu.VMEM((8, BLOCK), jnp.float32),
    ]
    return pl.pallas_call(
        tiles_kernel,
        out_shape=jax.ShapeDtypeStruct((owners, BLOCK // LANES, LANES), jnp.float32),
        in_specs=[
            pl.BlockSpec(memory_space=pltpu.SMEM),
            pl.BlockSpec(memory_space=pltpu.SMEM),
            pl.BlockSpec(memory_space=pltpu.VMEM),
        ],
        out_specs=pl.BlockSpec(memory_space=pltpu.VMEM),
        scratch_shapes=[pltpu.VMEM((8, ROW), jnp.float32)] * 2 + one * 2,
        compiler_params=pltpu.CompilerParams(vmem_limit_bytes=40 * 1024 * 1024),
    )(count, pairs, received)


def owned_kernel(picks_ref, returned_ref, out_ref):
    out_ref[...] = jnp.full(out_ref.shape, 4.0, jnp.float32)
    for t in range(returned_ref.shape[0]):
        which = picks_ref[t]
        out_ref[which] = jnp.minimum(out_ref[which], returned_ref[t])


def owned(picks, returned):
    return pl.pallas_call(
        owned_kernel,
        out_shape=jax.ShapeDtypeStruct((BLK_DEV,) + returned.shape[1:], jnp.float32),
        in_specs=[
            pl.BlockSpec(memory_space=pltpu.SMEM),
            pl.BlockSpec(memory_space=pltpu.VMEM),
        ],
        out_specs=pl.BlockSpec(memory_space=pltpu.VMEM),
    )(picks, returned)


def least_over_bands(mine):
    bands = lax.axis_size("band")
    others = [
        lax.ppermute(mine, "band", [(i, (i + step) % bands) for i in range(bands)])
        for step in range(1, bands)
    ]
    return functools.reduce(jnp.minimum, others, mine)


def local(series, block_pick, tile_pairs, tile_counts):
    picks = block_pick[0, 0]
    rows = rows_to_send(picks, series)
    received = lax.all_to_all(rows, "tile", split_axis=0, concat_axis=0, tiled=True)
    partial_value = tiles(tile_counts, tile_pairs[0, 0], received)
    returned = lax.all_to_all(partial_value, "tile", split_axis=0, concat_axis=0, tiled=True)
    return least_over_bands(owned(picks, returned)).reshape(BLK_DEV * BLOCK)


def solution(mesh):
    in_specs = (
        P("tile"),
        P("band", "tile", None),
        P("band", "tile", None, None),
        P("band", "tile"),
    )
    out_specs = P("tile")
    return jax.shard_map(local, mesh=mesh, in_specs=in_specs, out_specs=out_specs, check_vma=False)
```

```python
import functools

import jax
import jax.numpy as jnp
from jax import lax
from jax.experimental import pallas as pl
from jax.experimental.pallas import tpu as pltpu
from jax.sharding import PartitionSpec as P

SUBLEN = 64
BLOCK = 2048
BLK_DEV = 8
EXCL = 16
LANES = 128
ROW = BLOCK + LANES
ROW_TILES = ROW // LANES
CHUNK = 256
LEAST = -1.0 * SUBLEN


def rows_kernel(picks_ref, series_ref, out_ref, extra_ref):
    lane = lax.broadcasted_iota(jnp.int32, (1, LANES), 1)
    body = BLOCK // LANES
    first = lax.axis_index("tile") * BLK_DEV
    head = pltpu.roll(series_ref[0, 0:1], SUBLEN, 1)
    for which in range(BLK_DEV):
        after = series_ref[(which + 1) % BLK_DEV, 0:1]
        extra = jnp.where(lane < SUBLEN, after, head)
        number = (first + which).astype(jnp.float32)
        extra_ref[which : which + 1] = jnp.where(lane == LANES - 1, number, extra)
    for t in range(picks_ref.shape[0]):
        which = picks_ref[t]
        out_ref[t * ROW_TILES : t * ROW_TILES + body] = series_ref[which]
        out_ref[t * ROW_TILES + body : (t + 1) * ROW_TILES] = extra_ref[pl.ds(which, 1)]


def rows_to_send(picks, series):
    owners = picks.shape[0]
    rows = pl.pallas_call(
        rows_kernel,
        out_shape=jax.ShapeDtypeStruct((owners * ROW_TILES, LANES), jnp.float32),
        in_specs=[
            pl.BlockSpec(memory_space=pltpu.SMEM),
            pl.BlockSpec(memory_space=pltpu.VMEM),
        ],
        out_specs=pl.BlockSpec(memory_space=pltpu.VMEM),
        scratch_shapes=[pltpu.VMEM((BLK_DEV, LANES), jnp.float32)],
    )(picks, series.reshape(BLK_DEV, BLOCK // LANES, LANES))
    return rows.reshape(owners, 1, ROW)


def stage_row(recv_ref, owner, wide_ref):
    last = recv_ref.shape[0] - 1
    row = recv_ref[owner]
    extra = row[:, BLOCK:]
    number = jnp.broadcast_to(extra[:, LANES - 1 :], (1, LANES)).astype(jnp.int32)
    following = recv_ref[jnp.minimum(owner + 1, last)][:, BLOCK:]
    following = pltpu.roll(following, SUBLEN, 1)
    following = jnp.where(owner == last, 0.0, following)
    extra = jnp.where((number & (BLK_DEV - 1)) == BLK_DEV - 1, following, extra)
    wide = jnp.broadcast_to(jnp.concatenate([row[:, :BLOCK], extra], axis=1), (8, ROW))
    sub = lax.broadcasted_iota(jnp.int32, (8, ROW), 0)
    for bit in (1, 2, 4):
        wide = jnp.where((sub & bit) != 0, pltpu.roll(wide, ROW - bit, 1), wide)
    wide_ref[...] = wide
    return number


def window_chunk(wide_ref, n):
    size = CHUNK + LANES
    wide = wide_ref[:, n * CHUNK : n * CHUNK + size]
    parts = [wide[:, :CHUNK]]
    for a in range(1, SUBLEN // 8):
        parts.append(pltpu.roll(wide, size - 8 * a, 1)[:, :CHUNK])
    mean = jnp.sum(functools.reduce(jnp.add, parts), axis=0, keepdims=True) * (1.0 / SUBLEN)
    parts = [part - mean for part in parts]
    squares = functools.reduce(jnp.add, [part * part for part in parts])
    spread = jnp.sum(squares, axis=0, keepdims=True) * (1.0 / SUBLEN)
    inverse = lax.rsqrt(spread + 1e-05)
    znorm = jnp.concatenate([part * inverse for part in parts], axis=0)
    high = znorm.astype(jnp.bfloat16)
    low = (znorm - high.astype(jnp.float32)).astype(jnp.bfloat16)
    return high, low


def build_chunk(wide_rows, wide_cols, lhs, rhs, n):
    here = slice(n * CHUNK, (n + 1) * CHUNK)
    high, low = window_chunk(wide_cols, n)
    rhs[0:64, here] = high
    rhs[64:128, here] = low
    high, low = window_chunk(wide_rows, n)
    both = jnp.concatenate([high, low], axis=0)
    for q in range(CHUNK // LANES):
        part = both[:, q * LANES : (q + 1) * LANES].T
        at = slice(n * CHUNK + q * LANES, n * CHUNK + (q + 1) * LANES)
        lhs[at, 0:128] = part
        lhs[at, 128:256] = part


def excluded(products, a, b, ahead_ref):
    def masked(part, first_row, offset, ahead):
        gap = (
            offset + first_row
            + lax.broadcasted_iota(jnp.int32, part.shape, 0)
            - lax.broadcasted_iota(jnp.int32, part.shape, 1)
        )
        hit = jnp.logical_and(jnp.abs(gap) < EXCL, ahead_ref[0:1] == ahead)
        return jnp.where(hit, LEAST, part)

    if a == b:
        return masked(products, 0, 0, 0)
    last = BLOCK // LANES - 1
    if a - b in (1, -last):
        ahead = 0 if a - b == 1 else 1
        return jnp.concatenate([masked(products[:EXCL], 0, LANES, ahead), products[EXCL:]], axis=0)
    if a - b in (-1, last):
        ahead = 0 if a - b == -1 else -1
        top = LANES - EXCL
        return jnp.concatenate([products[:top], masked(products[top:], top, -LANES, ahead)], axis=0)
    return products


def multiply_chunk(lhs, rhs, ahead_ref, row_acc, col_acc, n):
    here = slice(n * CHUNK, (n + 1) * CHUNK)
    high, low = rhs[0:64, here], rhs[64:128, here]
    weights = jnp.concatenate([high, high, low, low], axis=0)
    halves = CHUNK // LANES
    best = [None] * halves
    products = jnp.dot(lhs[...], weights, preferred_element_type=jnp.float32)
    for a in range(BLOCK // LANES):
        at = slice(a * LANES, (a + 1) * LANES)
        strip = None
        for v in range(halves):
            b = n * halves + v
            block = excluded(products[at, v * LANES : (v + 1) * LANES], a, b, ahead_ref)
            strip = block if strip is None else jnp.maximum(strip, block)
            top = jnp.max(block.reshape(LANES // 8, 8, LANES), axis=0)
            best[v] = top if best[v] is None else jnp.maximum(best[v], top)
        row_acc[at] = strip if n == 0 else jnp.maximum(row_acc[at], strip)
    for v in range(halves):
        b = n * halves + v
        col_acc[:, b * LANES : (b + 1) * LANES] = best[v]


def finish_chunk(out_ref, first, second, row_acc, col_acc, n):
    for q in range(n * CHUNK // LANES, (n + 1) * CHUNK // LANES):
        at = slice(q * LANES, (q + 1) * LANES)
        most = jnp.max(row_acc[at].T, axis=0, keepdims=True)
        out_ref[first, q : q + 1] = jnp.minimum(out_ref[first, q : q + 1], 2.0 - most * (2.0 / SUBLEN))
        most = jnp.max(col_acc[:, at], axis=0, keepdims=True)
        out_ref[second, q : q + 1] = jnp.minimum(out_ref[second, q : q + 1], 2.0 - most * (2.0 / SUBLEN))


def tiles_kernel(count_ref, pairs_ref, recv_ref, out_ref, wide_rows, wide_cols, *buffers):
    sets = (buffers[:5], buffers[5:])
    count = count_ref[0, 0]
    out_ref[...] = jnp.full(out_ref.shape, 4.0, jnp.float32)
    for lhs, rhs, ahead, row_acc, col_acc in sets[1:]:
        row_acc[...] = jnp.full(row_acc.shape, LEAST, jnp.float32)
        col_acc[...] = jnp.full(col_acc.shape, LEAST, jnp.float32)

    def stage(s, ahead_ref):
        rows = stage_row(recv_ref, pairs_ref[0, s], wide_rows)
        cols = stage_row(recv_ref, pairs_ref[1, s], wide_cols)
        ahead_ref[...] = jnp.broadcast_to(rows - cols, ahead_ref.shape)

    stage(0, sets[0][2])
    for n in range(BLOCK // CHUNK):
        build_chunk(wide_rows, wide_cols, sets[0][0], sets[0][1], n)

    def phase(now, other, s):
        before = jnp.clip(s - 1, 0, count - 1)
        stage(jnp.minimum(s + 1, count - 1), other[2])
        for n in range(BLOCK // CHUNK):
            multiply_chunk(*now, n)
            build_chunk(wide_rows, wide_cols, other[0], other[1], n)
            finish_chunk(out_ref, pairs_ref[0, before], pairs_ref[1, before], other[3], other[4], n)

    def two(i, carry):
        phase(sets[0], sets[1], 2 * i)
        phase(sets[1], sets[0], 2 * i + 1)
        return carry

    steps = (count + 1) // 2
    lax.fori_loop(0, steps, two, 0)
    final = count - 1
    for n in range(BLOCK // CHUNK):
        finish_chunk(out_ref, pairs_ref[0, final], pairs_ref[1, final], sets[1][3], sets[1][4], n)


def tiles(count, pairs, received):
    owners = received.shape[0]
    one = [
        pltpu.VMEM((BLOCK, 256), jnp.bfloat16),
        pltpu.VMEM((2 * SUBLEN, BLOCK), jnp.bfloat16),
        pltpu.VMEM((8, LANES), jnp.int32),
        pltpu.VMEM((BLOCK, LANES), jnp.float32),
        pltpu.VMEM((8, BLOCK), jnp.float32),
    ]
    return pl.pallas_call(
        tiles_kernel,
        out_shape=jax.ShapeDtypeStruct((owners, BLOCK // LANES, LANES), jnp.float32),
        in_specs=[
            pl.BlockSpec(memory_space=pltpu.SMEM),
            pl.BlockSpec(memory_space=pltpu.SMEM),
            pl.BlockSpec(memory_space=pltpu.VMEM),
        ],
        out_specs=pl.BlockSpec(memory_space=pltpu.VMEM),
        scratch_shapes=[pltpu.VMEM((8, ROW), jnp.float32)] * 2 + one * 2,
        compiler_params=pltpu.CompilerParams(vmem_limit_bytes=40 * 1024 * 1024),
    )(count, pairs, received)


def owned_kernel(picks_ref, returned_ref, out_ref):
    out_ref[...] = jnp.full(out_ref.shape, 4.0, jnp.float32)
    for t in range(returned_ref.shape[0]):
        which = picks_ref[t]
        out_ref[which] = jnp.minimum(out_ref[which], returned_ref[t])


def owned(picks, returned):
    return pl.pallas_call(
        owned_kernel,
        out_shape=pltpu.VMEM((BLK_DEV,) + returned.shape[1:], jnp.float32),
        in_specs=[
            pl.BlockSpec(memory_space=pltpu.SMEM),
            pl.BlockSpec(memory_space=pltpu.VMEM),
        ],
        out_specs=pl.BlockSpec(memory_space=pltpu.VMEM),
    )(picks, returned)


def least_over_bands(mine):
    bands = lax.axis_size("band")
    others = [
        lax.ppermute(mine, "band", [(i, (i + step) % bands) for i in range(bands)])
        for step in range(1, bands)
    ]
    return functools.reduce(jnp.minimum, others, mine)


def local(series, block_pick, tile_pairs, tile_counts):
    picks = block_pick[0, 0]
    rows = rows_to_send(picks, series)
    rows, tile_counts, tile_pairs = lax.optimization_barrier((rows, tile_counts, tile_pairs))
    received = lax.all_to_all(rows, "tile", split_axis=0, concat_axis=0, tiled=True)
    partial_value = tiles(tile_counts, tile_pairs[0, 0], received)
    returned = lax.all_to_all(partial_value, "tile", split_axis=0, concat_axis=0, tiled=True)
    return least_over_bands(owned(picks, returned)).reshape(BLK_DEV * BLOCK)


def solution(mesh):
    in_specs = (
        P("tile"),
        P("band", "tile", None),
        P("band", "tile", None, None),
        P("band", "tile"),
    )
    out_specs = P("tile")
    return jax.shard_map(local, mesh=mesh, in_specs=in_specs, out_specs=out_specs, check_vma=False)
```

```python
import functools

import jax
import jax.numpy as jnp
from jax import lax
from jax.experimental import pallas as pl
from jax.experimental.pallas import tpu as pltpu
from jax.sharding import PartitionSpec as P

SUBLEN = 64
BLOCK = 2048
BLK_DEV = 8
EXCL = 16
LANES = 128
ROW = BLOCK + LANES
ROW_TILES = ROW // LANES
CHUNK = 256
LEAST = -1.0 * SUBLEN


def rows_kernel(picks_ref, series_ref, out_ref, extra_ref):
    lane = lax.broadcasted_iota(jnp.int32, (1, LANES), 1)
    body = BLOCK // LANES
    first = lax.axis_index("tile") * BLK_DEV
    head = pltpu.roll(series_ref[0, 0:1], SUBLEN, 1)
    for which in range(BLK_DEV):
        after = series_ref[(which + 1) % BLK_DEV, 0:1]
        extra = jnp.where(lane < SUBLEN, after, head)
        number = (first + which).astype(jnp.float32)
        extra_ref[which : which + 1] = jnp.where(lane == LANES - 1, number, extra)
    for t in range(picks_ref.shape[0]):
        which = picks_ref[t]
        out_ref[t * ROW_TILES : t * ROW_TILES + body] = series_ref[which]
        out_ref[t * ROW_TILES + body : (t + 1) * ROW_TILES] = extra_ref[pl.ds(which, 1)]


def rows_to_send(picks, series):
    owners = picks.shape[0]
    rows = pl.pallas_call(
        rows_kernel,
        out_shape=jax.ShapeDtypeStruct((owners * ROW_TILES, LANES), jnp.float32),
        in_specs=[
            pl.BlockSpec(memory_space=pltpu.SMEM),
            pl.BlockSpec(memory_space=pltpu.VMEM),
        ],
        out_specs=pl.BlockSpec(memory_space=pltpu.VMEM),
        scratch_shapes=[pltpu.VMEM((BLK_DEV, LANES), jnp.float32)],
    )(picks, series.reshape(BLK_DEV, BLOCK // LANES, LANES))
    return rows.reshape(owners, 1, ROW)


def stage_row(recv_ref, owner, wide_ref):
    last = recv_ref.shape[0] - 1
    row = recv_ref[owner]
    extra = row[:, BLOCK:]
    number = jnp.broadcast_to(extra[:, LANES - 1 :], (1, LANES)).astype(jnp.int32)
    following = recv_ref[jnp.minimum(owner + 1, last)][:, BLOCK:]
    following = pltpu.roll(following, SUBLEN, 1)
    following = jnp.where(owner == last, 0.0, following)
    extra = jnp.where((number & (BLK_DEV - 1)) == BLK_DEV - 1, following, extra)
    wide = jnp.broadcast_to(jnp.concatenate([row[:, :BLOCK], extra], axis=1), (8, ROW))
    sub = lax.broadcasted_iota(jnp.int32, (8, ROW), 0)
    for bit in (1, 2, 4):
        wide = jnp.where((sub & bit) != 0, pltpu.roll(wide, ROW - bit, 1), wide)
    wide_ref[...] = wide
    return number


def window_chunk(wide_ref, n):
    size = CHUNK + LANES
    wide = wide_ref[:, n * CHUNK : n * CHUNK + size]
    parts = [wide[:, :CHUNK]]
    for a in range(1, SUBLEN // 8):
        parts.append(pltpu.roll(wide, size - 8 * a, 1)[:, :CHUNK])
    mean = jnp.sum(functools.reduce(jnp.add, parts), axis=0, keepdims=True) * (1.0 / SUBLEN)
    parts = [part - mean for part in parts]
    squares = functools.reduce(jnp.add, [part * part for part in parts])
    spread = jnp.sum(squares, axis=0, keepdims=True) * (1.0 / SUBLEN)
    inverse = lax.rsqrt(spread + 1e-05)
    znorm = jnp.concatenate([part * inverse for part in parts], axis=0)
    high = znorm.astype(jnp.bfloat16)
    low = (znorm - high.astype(jnp.float32)).astype(jnp.bfloat16)
    return high, low


def build_chunk(wide_rows, wide_cols, lhs, rhs, n):
    here = slice(n * CHUNK, (n + 1) * CHUNK)
    high, low = window_chunk(wide_cols, n)
    rhs[0:64, here] = high
    rhs[64:128, here] = low
    high, low = window_chunk(wide_rows, n)
    both = jnp.concatenate([high, low], axis=0)
    for q in range(CHUNK // LANES):
        part = both[:, q * LANES : (q + 1) * LANES].T
        at = slice(n * CHUNK + q * LANES, n * CHUNK + (q + 1) * LANES)
        lhs[at, 0:128] = part
        lhs[at, 128:256] = part


def excluded(products, a, b, ahead_ref):
    def masked(part, first_row, offset, ahead):
        gap = (
            offset + first_row
            + lax.broadcasted_iota(jnp.int32, part.shape, 0)
            - lax.broadcasted_iota(jnp.int32, part.shape, 1)
        )
        hit = jnp.logical_and(jnp.abs(gap) < EXCL, ahead_ref[0:1] == ahead)
        return jnp.where(hit, LEAST, part)

    if a == b:
        return masked(products, 0, 0, 0)
    last = BLOCK // LANES - 1
    if a - b in (1, -last):
        ahead = 0 if a - b == 1 else 1
        return jnp.concatenate([masked(products[:EXCL], 0, LANES, ahead), products[EXCL:]], axis=0)
    if a - b in (-1, last):
        ahead = 0 if a - b == -1 else -1
        top = LANES - EXCL
        return jnp.concatenate([products[:top], masked(products[top:], top, -LANES, ahead)], axis=0)
    return products


def multiply_chunk(lhs, rhs, ahead_ref, row_acc, col_acc, n):
    here = slice(n * CHUNK, (n + 1) * CHUNK)
    high, low = rhs[0:64, here], rhs[64:128, here]
    weights = jnp.concatenate([high, high, low, low], axis=0)
    halves = CHUNK // LANES
    best = [None] * halves
    products = jnp.dot(lhs[...], weights, preferred_element_type=jnp.float32)
    for a in range(BLOCK // LANES):
        at = slice(a * LANES, (a + 1) * LANES)
        strip = None
        for v in range(halves):
            b = n * halves + v
            block = excluded(products[at, v * LANES : (v + 1) * LANES], a, b, ahead_ref)
            strip = block if strip is None else jnp.maximum(strip, block)
            top = jnp.max(block.reshape(LANES // 8, 8, LANES), axis=0)
            best[v] = top if best[v] is None else jnp.maximum(best[v], top)
        row_acc[at] = strip if n == 0 else jnp.maximum(row_acc[at], strip)
    for v in range(halves):
        b = n * halves + v
        col_acc[:, b * LANES : (b + 1) * LANES] = best[v]


def finish_chunk(out_ref, first, second, row_acc, col_acc, n):
    for q in range(n * CHUNK // LANES, (n + 1) * CHUNK // LANES):
        at = slice(q * LANES, (q + 1) * LANES)
        most = jnp.max(row_acc[at].T, axis=0, keepdims=True)
        out_ref[first, q : q + 1] = jnp.minimum(out_ref[first, q : q + 1], 2.0 - most * (2.0 / SUBLEN))
        most = jnp.max(col_acc[:, at], axis=0, keepdims=True)
        out_ref[second, q : q + 1] = jnp.minimum(out_ref[second, q : q + 1], 2.0 - most * (2.0 / SUBLEN))


def tiles_kernel(count_ref, pairs_ref, recv_ref, out_ref, wide_rows, wide_cols, *buffers):
    sets = (buffers[:5], buffers[5:])
    count = count_ref[0, 0]
    out_ref[...] = jnp.full(out_ref.shape, 4.0, jnp.float32)
    for lhs, rhs, ahead, row_acc, col_acc in sets[1:]:
        row_acc[...] = jnp.full(row_acc.shape, LEAST, jnp.float32)
        col_acc[...] = jnp.full(col_acc.shape, LEAST, jnp.float32)

    def stage(s, ahead_ref):
        rows = stage_row(recv_ref, pairs_ref[0, s], wide_rows)
        cols = stage_row(recv_ref, pairs_ref[1, s], wide_cols)
        ahead_ref[...] = jnp.broadcast_to(rows - cols, ahead_ref.shape)

    stage(0, sets[0][2])
    for n in range(BLOCK // CHUNK):
        build_chunk(wide_rows, wide_cols, sets[0][0], sets[0][1], n)

    def phase(now, other, s):
        before = jnp.clip(s - 1, 0, count - 1)
        stage(jnp.minimum(s + 1, count - 1), other[2])
        for n in range(BLOCK // CHUNK):
            multiply_chunk(*now, n)
            build_chunk(wide_rows, wide_cols, other[0], other[1], n)
            finish_chunk(out_ref, pairs_ref[0, before], pairs_ref[1, before], other[3], other[4], n)

    def two(i, carry):
        phase(sets[0], sets[1], 2 * i)
        phase(sets[1], sets[0], 2 * i + 1)
        return carry

    steps = (count + 1) // 2
    lax.fori_loop(0, steps, two, 0)
    final = count - 1
    for n in range(BLOCK // CHUNK):
        finish_chunk(out_ref, pairs_ref[0, final], pairs_ref[1, final], sets[1][3], sets[1][4], n)


def tiles(count, pairs, received):
    owners = received.shape[0]
    one = [
        pltpu.VMEM((BLOCK, 256), jnp.bfloat16),
        pltpu.VMEM((2 * SUBLEN, BLOCK), jnp.bfloat16),
        pltpu.VMEM((8, LANES), jnp.int32),
        pltpu.VMEM((BLOCK, LANES), jnp.float32),
        pltpu.VMEM((8, BLOCK), jnp.float32),
    ]
    return pl.pallas_call(
        tiles_kernel,
        out_shape=jax.ShapeDtypeStruct((owners, BLOCK // LANES, LANES), jnp.float32),
        in_specs=[
            pl.BlockSpec(memory_space=pltpu.SMEM),
            pl.BlockSpec(memory_space=pltpu.SMEM),
            pl.BlockSpec(memory_space=pltpu.VMEM),
        ],
        out_specs=pl.BlockSpec(memory_space=pltpu.VMEM),
        scratch_shapes=[pltpu.VMEM((8, ROW), jnp.float32)] * 2 + one * 2,
        compiler_params=pltpu.CompilerParams(vmem_limit_bytes=40 * 1024 * 1024),
    )(count, pairs, received)


def owned_kernel(picks_ref, returned_ref, out_ref):
    out_ref[...] = jnp.full(out_ref.shape, 4.0, jnp.float32)
    for t in range(returned_ref.shape[0]):
        which = picks_ref[t]
        out_ref[which] = jnp.minimum(out_ref[which], returned_ref[t])


def owned(picks, returned):
    return pl.pallas_call(
        owned_kernel,
        out_shape=pltpu.VMEM((BLK_DEV,) + returned.shape[1:], jnp.float32),
        in_specs=[
            pl.BlockSpec(memory_space=pltpu.SMEM),
            pl.BlockSpec(memory_space=pltpu.VMEM),
        ],
        out_specs=pl.BlockSpec(memory_space=pltpu.VMEM),
    )(picks, pltpu.with_memory_space_constraint(returned, pltpu.VMEM))


def least_over_bands(mine):
    bands = lax.axis_size("band")
    others = [
        lax.ppermute(mine, "band", [(i, (i + step) % bands) for i in range(bands)])
        for step in range(1, bands)
    ]
    return functools.reduce(jnp.minimum, others, mine)


def local(series, block_pick, tile_pairs, tile_counts):
    picks = block_pick[0, 0]
    rows = rows_to_send(picks, series)
    rows, tile_counts, tile_pairs = lax.optimization_barrier((rows, tile_counts, tile_pairs))
    received = lax.all_to_all(rows, "tile", split_axis=0, concat_axis=0, tiled=True)
    partial_value = tiles(tile_counts, tile_pairs[0, 0], received)
    returned = lax.all_to_all(partial_value, "tile", split_axis=0, concat_axis=0, tiled=True)
    return least_over_bands(owned(picks, returned)).reshape(BLK_DEV * BLOCK)


def solution(mesh):
    in_specs = (
        P("tile"),
        P("band", "tile", None),
        P("band", "tile", None, None),
        P("band", "tile"),
    )
    out_specs = P("tile")
    return jax.shard_map(local, mesh=mesh, in_specs=in_specs, out_specs=out_specs, check_vma=False)
```

```python
import functools

import jax
import jax.numpy as jnp
from jax import lax
from jax.experimental import pallas as pl
from jax.experimental.pallas import tpu as pltpu
from jax.sharding import PartitionSpec as P

SUBLEN = 64
BLOCK = 2048
BLK_DEV = 8
EXCL = 16
LANES = 128
ROW = BLOCK + LANES
ROW_TILES = ROW // LANES
CHUNK = 256
LEAST = -1.0 * SUBLEN


def rows_kernel(picks_ref, series_ref, out_ref, extra_ref):
    lane = lax.broadcasted_iota(jnp.int32, (1, LANES), 1)
    body = BLOCK // LANES
    first = lax.axis_index("tile") * BLK_DEV
    head = pltpu.roll(series_ref[0, 0:1], SUBLEN, 1)
    for which in range(BLK_DEV):
        after = series_ref[(which + 1) % BLK_DEV, 0:1]
        extra = jnp.where(lane < SUBLEN, after, head)
        number = (first + which).astype(jnp.float32)
        extra_ref[which : which + 1] = jnp.where(lane == LANES - 1, number, extra)
    for t in range(picks_ref.shape[0]):
        which = picks_ref[t]
        out_ref[t * ROW_TILES : t * ROW_TILES + body] = series_ref[which]
        out_ref[t * ROW_TILES + body : (t + 1) * ROW_TILES] = extra_ref[pl.ds(which, 1)]


def rows_to_send(picks, series):
    owners = picks.shape[0]
    rows = pl.pallas_call(
        rows_kernel,
        out_shape=jax.ShapeDtypeStruct((owners * ROW_TILES, LANES), jnp.float32),
        in_specs=[
            pl.BlockSpec(memory_space=pltpu.SMEM),
            pl.BlockSpec(memory_space=pltpu.VMEM),
        ],
        out_specs=pl.BlockSpec(memory_space=pltpu.VMEM),
        scratch_shapes=[pltpu.VMEM((BLK_DEV, LANES), jnp.float32)],
    )(picks, series.reshape(BLK_DEV, BLOCK // LANES, LANES))
    return rows.reshape(owners, 1, ROW)


def stage_row(recv_ref, owner, wide_ref):
    last = recv_ref.shape[0] - 1
    row = recv_ref[owner]
    extra = row[:, BLOCK:]
    number = jnp.broadcast_to(extra[:, LANES - 1 :], (1, LANES)).astype(jnp.int32)
    following = recv_ref[jnp.minimum(owner + 1, last)][:, BLOCK:]
    following = pltpu.roll(following, SUBLEN, 1)
    following = jnp.where(owner == last, 0.0, following)
    extra = jnp.where((number & (BLK_DEV - 1)) == BLK_DEV - 1, following, extra)
    wide = jnp.broadcast_to(jnp.concatenate([row[:, :BLOCK], extra], axis=1), (8, ROW))
    sub = lax.broadcasted_iota(jnp.int32, (8, ROW), 0)
    for bit in (1, 2, 4):
        wide = jnp.where((sub & bit) != 0, pltpu.roll(wide, ROW - bit, 1), wide)
    wide_ref[...] = wide
    return number


def window_chunk(wide_ref, n):
    size = CHUNK + LANES
    wide = wide_ref[:, n * CHUNK : n * CHUNK + size]
    parts = [wide[:, :CHUNK]]
    for a in range(1, SUBLEN // 8):
        parts.append(pltpu.roll(wide, size - 8 * a, 1)[:, :CHUNK])
    mean = jnp.sum(functools.reduce(jnp.add, parts), axis=0, keepdims=True) * (1.0 / SUBLEN)
    parts = [part - mean for part in parts]
    squares = functools.reduce(jnp.add, [part * part for part in parts])
    spread = jnp.sum(squares, axis=0, keepdims=True) * (1.0 / SUBLEN)
    inverse = lax.rsqrt(spread + 1e-05)
    znorm = jnp.concatenate([part * inverse for part in parts], axis=0)
    high = znorm.astype(jnp.bfloat16)
    low = (znorm - high.astype(jnp.float32)).astype(jnp.bfloat16)
    return high, low


def build_chunk(wide_rows, wide_cols, lhs, rhs, n):
    here = slice(n * CHUNK, (n + 1) * CHUNK)
    high, low = window_chunk(wide_cols, n)
    rhs[0:64, here] = high
    rhs[64:128, here] = low
    high, low = window_chunk(wide_rows, n)
    both = jnp.concatenate([high, low], axis=0)
    for q in range(CHUNK // LANES):
        part = both[:, q * LANES : (q + 1) * LANES].T
        at = slice(n * CHUNK + q * LANES, n * CHUNK + (q + 1) * LANES)
        lhs[at, 0:128] = part
        lhs[at, 128:256] = part


def excluded(products, a, b, ahead_ref):
    def masked(part, first_row, offset, ahead):
        gap = (
            offset + first_row
            + lax.broadcasted_iota(jnp.int32, part.shape, 0)
            - lax.broadcasted_iota(jnp.int32, part.shape, 1)
        )
        hit = jnp.logical_and(jnp.abs(gap) < EXCL, ahead_ref[0:1] == ahead)
        return jnp.where(hit, LEAST, part)

    if a == b:
        return masked(products, 0, 0, 0)
    last = BLOCK // LANES - 1
    if a - b in (1, -last):
        ahead = 0 if a - b == 1 else 1
        return jnp.concatenate([masked(products[:EXCL], 0, LANES, ahead), products[EXCL:]], axis=0)
    if a - b in (-1, last):
        ahead = 0 if a - b == -1 else -1
        top = LANES - EXCL
        return jnp.concatenate([products[:top], masked(products[top:], top, -LANES, ahead)], axis=0)
    return products


def multiply_chunk(lhs, rhs, ahead_ref, row_acc, col_acc, n):
    here = slice(n * CHUNK, (n + 1) * CHUNK)
    high, low = rhs[0:64, here], rhs[64:128, here]
    weights = jnp.concatenate([high, high, low, low], axis=0)
    halves = CHUNK // LANES
    best = [None] * halves
    products = jnp.dot(lhs[...], weights, preferred_element_type=jnp.float32)
    for a in range(BLOCK // LANES):
        at = slice(a * LANES, (a + 1) * LANES)
        strip = None
        for v in range(halves):
            b = n * halves + v
            block = excluded(products[at, v * LANES : (v + 1) * LANES], a, b, ahead_ref)
            strip = block if strip is None else jnp.maximum(strip, block)
            top = jnp.max(block.reshape(LANES // 8, 8, LANES), axis=0)
            best[v] = top if best[v] is None else jnp.maximum(best[v], top)
        row_acc[at] = strip if n == 0 else jnp.maximum(row_acc[at], strip)
    for v in range(halves):
        b = n * halves + v
        col_acc[:, b * LANES : (b + 1) * LANES] = best[v]


def finish_chunk(out_ref, first, second, row_acc, col_acc, n):
    for q in range(n * CHUNK // LANES, (n + 1) * CHUNK // LANES):
        at = slice(q * LANES, (q + 1) * LANES)
        most = jnp.max(row_acc[at].T, axis=0, keepdims=True)
        out_ref[first, q : q + 1] = jnp.minimum(out_ref[first, q : q + 1], 2.0 - most * (2.0 / SUBLEN))
        most = jnp.max(col_acc[:, at], axis=0, keepdims=True)
        out_ref[second, q : q + 1] = jnp.minimum(out_ref[second, q : q + 1], 2.0 - most * (2.0 / SUBLEN))


def tiles_kernel(count_ref, pairs_ref, recv_ref, out_ref, wide_rows, wide_cols, *buffers):
    sets = (buffers[:5], buffers[5:])
    count = count_ref[0, 0]
    out_ref[...] = jnp.full(out_ref.shape, 4.0, jnp.float32)
    for lhs, rhs, ahead, row_acc, col_acc in sets[1:]:
        row_acc[...] = jnp.full(row_acc.shape, LEAST, jnp.float32)
        col_acc[...] = jnp.full(col_acc.shape, LEAST, jnp.float32)

    def stage(s, ahead_ref):
        rows = stage_row(recv_ref, pairs_ref[0, s], wide_rows)
        cols = stage_row(recv_ref, pairs_ref[1, s], wide_cols)
        ahead_ref[...] = jnp.broadcast_to(rows - cols, ahead_ref.shape)

    stage(0, sets[0][2])
    for n in range(BLOCK // CHUNK):
        build_chunk(wide_rows, wide_cols, sets[0][0], sets[0][1], n)

    def phase(now, other, s):
        before = jnp.clip(s - 1, 0, count - 1)
        stage(jnp.minimum(s + 1, count - 1), other[2])
        for n in range(BLOCK // CHUNK):
            multiply_chunk(*now, n)
            build_chunk(wide_rows, wide_cols, other[0], other[1], n)
            finish_chunk(out_ref, pairs_ref[0, before], pairs_ref[1, before], other[3], other[4], n)

    def two(i, carry):
        phase(sets[0], sets[1], 2 * i)
        phase(sets[1], sets[0], 2 * i + 1)
        return carry

    steps = (count + 1) // 2
    lax.fori_loop(0, steps, two, 0)
    final = count - 1
    for n in range(BLOCK // CHUNK):
        finish_chunk(out_ref, pairs_ref[0, final], pairs_ref[1, final], sets[1][3], sets[1][4], n)


def tiles(count, pairs, received):
    owners = received.shape[0]
    one = [
        pltpu.VMEM((BLOCK, 256), jnp.bfloat16),
        pltpu.VMEM((2 * SUBLEN, BLOCK), jnp.bfloat16),
        pltpu.VMEM((8, LANES), jnp.int32),
        pltpu.VMEM((BLOCK, LANES), jnp.float32),
        pltpu.VMEM((8, BLOCK), jnp.float32),
    ]
    return pl.pallas_call(
        tiles_kernel,
        out_shape=jax.ShapeDtypeStruct((owners, BLOCK // LANES, LANES), jnp.float32),
        in_specs=[
            pl.BlockSpec(memory_space=pltpu.SMEM),
            pl.BlockSpec(memory_space=pltpu.SMEM),
            pl.BlockSpec(memory_space=pltpu.VMEM),
        ],
        out_specs=pl.BlockSpec(memory_space=pltpu.VMEM),
        scratch_shapes=[pltpu.VMEM((8, ROW), jnp.float32)] * 2 + one * 2,
        compiler_params=pltpu.CompilerParams(vmem_limit_bytes=40 * 1024 * 1024),
    )(count, pairs, received)


def owned_kernel(picks_ref, returned_ref, out_ref):
    out_ref[...] = jnp.full(out_ref.shape, 4.0, jnp.float32)
    for t in range(returned_ref.shape[0]):
        which = picks_ref[t]
        out_ref[which] = jnp.minimum(out_ref[which], returned_ref[t])


def owned(picks, returned):
    return pl.pallas_call(
        owned_kernel,
        out_shape=pltpu.VMEM((BLK_DEV,) + returned.shape[1:], jnp.float32),
        in_specs=[
            pl.BlockSpec(memory_space=pltpu.SMEM),
            pl.BlockSpec(memory_space=pltpu.VMEM),
        ],
        out_specs=pl.BlockSpec(memory_space=pltpu.VMEM),
    )(
        pltpu.with_memory_space_constraint(picks, pltpu.VMEM),
        pltpu.with_memory_space_constraint(returned, pltpu.VMEM),
    )


def least_over_bands(mine):
    bands = lax.axis_size("band")
    others = [
        lax.ppermute(mine, "band", [(i, (i + step) % bands) for i in range(bands)])
        for step in range(1, bands)
    ]
    return functools.reduce(jnp.minimum, others, mine)


def local(series, block_pick, tile_pairs, tile_counts):
    picks = block_pick[0, 0]
    rows = rows_to_send(picks, series)
    rows, tile_counts, tile_pairs = lax.optimization_barrier((rows, tile_counts, tile_pairs))
    received = lax.all_to_all(rows, "tile", split_axis=0, concat_axis=0, tiled=True)
    partial_value = tiles(tile_counts, tile_pairs[0, 0], received)
    returned = lax.all_to_all(partial_value, "tile", split_axis=0, concat_axis=0, tiled=True)
    return least_over_bands(owned(picks, returned)).reshape(BLK_DEV * BLOCK)


def solution(mesh):
    in_specs = (
        P("tile"),
        P("band", "tile", None),
        P("band", "tile", None, None),
        P("band", "tile"),
    )
    out_specs = P("tile")
    return jax.shard_map(local, mesh=mesh, in_specs=in_specs, out_specs=out_specs, check_vma=False)
```

```python
import functools

import jax
import jax.numpy as jnp
from jax import lax
from jax.experimental import pallas as pl
from jax.experimental.pallas import tpu as pltpu
from jax.sharding import PartitionSpec as P

SUBLEN = 64
BLOCK = 2048
BLK_DEV = 8
EXCL = 16
LANES = 128
ROW = BLOCK + LANES
ROW_TILES = ROW // LANES
CHUNK = 256
LEAD = 2
LEAST = -1.0 * SUBLEN


def rows_kernel(picks_ref, series_ref, out_ref, extra_ref):
    lane = lax.broadcasted_iota(jnp.int32, (1, LANES), 1)
    body = BLOCK // LANES
    first = lax.axis_index("tile") * BLK_DEV
    head = pltpu.roll(series_ref[0, 0:1], SUBLEN, 1)
    for which in range(BLK_DEV):
        after = series_ref[(which + 1) % BLK_DEV, 0:1]
        extra = jnp.where(lane < SUBLEN, after, head)
        number = (first + which).astype(jnp.float32)
        extra_ref[which : which + 1] = jnp.where(lane == LANES - 1, number, extra)
    for t in range(picks_ref.shape[0]):
        which = picks_ref[t]
        out_ref[t * ROW_TILES : t * ROW_TILES + body] = series_ref[which]
        out_ref[t * ROW_TILES + body : (t + 1) * ROW_TILES] = extra_ref[pl.ds(which, 1)]


def rows_to_send(picks, series):
    owners = picks.shape[0]
    rows = pl.pallas_call(
        rows_kernel,
        out_shape=jax.ShapeDtypeStruct((owners * ROW_TILES, LANES), jnp.float32),
        in_specs=[
            pl.BlockSpec(memory_space=pltpu.SMEM),
            pl.BlockSpec(memory_space=pltpu.VMEM),
        ],
        out_specs=pl.BlockSpec(memory_space=pltpu.VMEM),
        scratch_shapes=[pltpu.VMEM((BLK_DEV, LANES), jnp.float32)],
    )(picks, series.reshape(BLK_DEV, BLOCK // LANES, LANES))
    return rows.reshape(owners, 1, ROW)


def stage_row(recv_ref, owner, wide_ref):
    last = recv_ref.shape[0] - 1
    row = recv_ref[owner]
    extra = row[:, BLOCK:]
    number = jnp.broadcast_to(extra[:, LANES - 1 :], (1, LANES)).astype(jnp.int32)
    following = recv_ref[jnp.minimum(owner + 1, last)][:, BLOCK:]
    following = pltpu.roll(following, SUBLEN, 1)
    following = jnp.where(owner == last, 0.0, following)
    extra = jnp.where((number & (BLK_DEV - 1)) == BLK_DEV - 1, following, extra)
    wide = jnp.broadcast_to(jnp.concatenate([row[:, :BLOCK], extra], axis=1), (8, ROW))
    sub = lax.broadcasted_iota(jnp.int32, (8, ROW), 0)
    for bit in (1, 2, 4):
        wide = jnp.where((sub & bit) != 0, pltpu.roll(wide, ROW - bit, 1), wide)
    wide_ref[...] = wide
    return number


def window_chunk(wide_ref, n):
    size = CHUNK + LANES
    wide = wide_ref[:, n * CHUNK : n * CHUNK + size]
    parts = [wide[:, :CHUNK]]
    for a in range(1, SUBLEN // 8):
        parts.append(pltpu.roll(wide, size - 8 * a, 1)[:, :CHUNK])
    mean = jnp.sum(functools.reduce(jnp.add, parts), axis=0, keepdims=True) * (1.0 / SUBLEN)
    parts = [part - mean for part in parts]
    squares = functools.reduce(jnp.add, [part * part for part in parts])
    spread = jnp.sum(squares, axis=0, keepdims=True) * (1.0 / SUBLEN)
    inverse = lax.rsqrt(spread + 1e-05)
    znorm = jnp.concatenate([part * inverse for part in parts], axis=0)
    high = znorm.astype(jnp.bfloat16)
    low = (znorm - high.astype(jnp.float32)).astype(jnp.bfloat16)
    return high, low


def build_cols(wide_cols, rhs, n):
    here = slice(n * CHUNK, (n + 1) * CHUNK)
    high, low = window_chunk(wide_cols, n)
    rhs[0:64, here] = high
    rhs[64:128, here] = low


def build_rows(wide_rows, lhs, n):
    high, low = window_chunk(wide_rows, n)
    both = jnp.concatenate([high, low], axis=0)
    for q in range(CHUNK // LANES):
        part = both[:, q * LANES : (q + 1) * LANES].T
        at = slice(n * CHUNK + q * LANES, n * CHUNK + (q + 1) * LANES)
        lhs[at, 0:128] = part
        lhs[at, 128:256] = part


def excluded(products, a, b, ahead_ref):
    def masked(part, first_row, offset, ahead):
        gap = (
            offset + first_row
            + lax.broadcasted_iota(jnp.int32, part.shape, 0)
            - lax.broadcasted_iota(jnp.int32, part.shape, 1)
        )
        hit = jnp.logical_and(jnp.abs(gap) < EXCL, ahead_ref[0:1] == ahead)
        return jnp.where(hit, LEAST, part)

    if a == b:
        return masked(products, 0, 0, 0)
    last = BLOCK // LANES - 1
    if a - b in (1, -last):
        ahead = 0 if a - b == 1 else 1
        return jnp.concatenate([masked(products[:EXCL], 0, LANES, ahead), products[EXCL:]], axis=0)
    if a - b in (-1, last):
        ahead = 0 if a - b == -1 else -1
        top = LANES - EXCL
        return jnp.concatenate([products[:top], masked(products[top:], top, -LANES, ahead)], axis=0)
    return products


def multiply_chunk(lhs, rhs, wide_cols, ahead_ref, row_acc, n):
    here = slice(n * CHUNK, (n + 1) * CHUNK)
    high, low = rhs[0:64, here], rhs[64:128, here]
    weights = jnp.concatenate([high, high, low, low], axis=0)
    halves = CHUNK // LANES
    best = [None] * halves
    products = jnp.dot(lhs[...], weights, preferred_element_type=jnp.float32)
    for a in range(BLOCK // LANES):
        at = slice(a * LANES, (a + 1) * LANES)
        strip = None
        for v in range(halves):
            b = n * halves + v
            block = excluded(products[at, v * LANES : (v + 1) * LANES], a, b, ahead_ref)
            strip = block if strip is None else jnp.maximum(strip, block)
            top = jnp.max(block.reshape(LANES // 8, 8, LANES), axis=0)
            best[v] = top if best[v] is None else jnp.maximum(best[v], top)
        row_acc[at] = strip if n == 0 else jnp.maximum(row_acc[at], strip)
    return best


def least_distance(most):
    return 2.0 - most * (2.0 / SUBLEN)


def finish_cols(out_ref, second, best, n):
    for v, top in enumerate(best):
        q = n * (CHUNK // LANES) + v
        least = least_distance(jnp.max(top, axis=0, keepdims=True))
        out_ref[second, q : q + 1] = jnp.minimum(out_ref[second, q : q + 1], least)


def finish_rows(out_ref, first, row_acc, n):
    for q in range(n * CHUNK // LANES, (n + 1) * CHUNK // LANES):
        most = jnp.max(row_acc[q * LANES : (q + 1) * LANES].T, axis=0, keepdims=True)
        out_ref[first, q : q + 1] = jnp.minimum(out_ref[first, q : q + 1], least_distance(most))


def tiles_kernel(count_ref, pairs_ref, recv_ref, out_ref, wide_rows, *buffers):
    sets = (buffers[:5], buffers[5:])
    count = count_ref[0, 0]
    chunks = BLOCK // CHUNK
    out_ref[...] = jnp.full(out_ref.shape, 4.0, jnp.float32)
    sets[1][4][...] = jnp.full(sets[1][4].shape, LEAST, jnp.float32)

    def stage(s, into):
        rows = stage_row(recv_ref, pairs_ref[0, s], wide_rows)
        cols = stage_row(recv_ref, pairs_ref[1, s], into[2])
        into[3][...] = jnp.broadcast_to(rows - cols, into[3].shape)

    stage(0, sets[0])
    for n in range(chunks):
        build_rows(wide_rows, sets[0][0], n)
    for n in range(LEAD):
        build_cols(sets[0][2], sets[0][1], n)

    def phase(now, other, s):
        before = jnp.clip(s - 1, 0, count - 1)
        second = pairs_ref[1, jnp.minimum(s, count - 1)]
        stage(jnp.minimum(s + 1, count - 1), other)
        for n in range(chunks):
            best = multiply_chunk(*now, n)
            ahead = now if n + LEAD < chunks else other
            build_cols(ahead[2], ahead[1], (n + LEAD) % chunks)
            build_rows(wide_rows, other[0], n)
            finish_rows(out_ref, pairs_ref[0, before], other[4], n)
            finish_cols(out_ref, second, best, n)

    def two(i, carry):
        phase(sets[0], sets[1], 2 * i)
        phase(sets[1], sets[0], 2 * i + 1)
        return carry

    lax.fori_loop(0, (count + 1) // 2, two, 0)
    for n in range(chunks):
        finish_rows(out_ref, pairs_ref[0, count - 1], sets[1][4], n)


def tiles(count, pairs, received):
    owners = received.shape[0]
    one = [
        pltpu.VMEM((BLOCK, 256), jnp.bfloat16),
        pltpu.VMEM((2 * SUBLEN, BLOCK), jnp.bfloat16),
        pltpu.VMEM((8, ROW), jnp.float32),
        pltpu.VMEM((8, LANES), jnp.int32),
        pltpu.VMEM((BLOCK, LANES), jnp.float32),
    ]
    return pl.pallas_call(
        tiles_kernel,
        out_shape=jax.ShapeDtypeStruct((owners, BLOCK // LANES, LANES), jnp.float32),
        in_specs=[
            pl.BlockSpec(memory_space=pltpu.SMEM),
            pl.BlockSpec(memory_space=pltpu.SMEM),
            pl.BlockSpec(memory_space=pltpu.VMEM),
        ],
        out_specs=pl.BlockSpec(memory_space=pltpu.VMEM),
        scratch_shapes=[pltpu.VMEM((8, ROW), jnp.float32)] + one * 2,
        compiler_params=pltpu.CompilerParams(vmem_limit_bytes=40 * 1024 * 1024),
    )(count, pairs, received)


def owned_kernel(picks_ref, returned_ref, out_ref):
    out_ref[...] = jnp.full(out_ref.shape, 4.0, jnp.float32)
    for t in range(returned_ref.shape[0]):
        which = picks_ref[t]
        out_ref[which] = jnp.minimum(out_ref[which], returned_ref[t])


def owned(picks, returned):
    return pl.pallas_call(
        owned_kernel,
        out_shape=pltpu.VMEM((BLK_DEV,) + returned.shape[1:], jnp.float32),
        in_specs=[
            pl.BlockSpec(memory_space=pltpu.SMEM),
            pl.BlockSpec(memory_space=pltpu.VMEM),
        ],
        out_specs=pl.BlockSpec(memory_space=pltpu.VMEM),
    )(
        pltpu.with_memory_space_constraint(picks, pltpu.VMEM),
        pltpu.with_memory_space_constraint(returned, pltpu.VMEM),
    )


def least_over_bands(mine):
    bands = lax.axis_size("band")
    others = [
        lax.ppermute(mine, "band", [(i, (i + step) % bands) for i in range(bands)])
        for step in range(1, bands)
    ]
    return functools.reduce(jnp.minimum, others, mine)


def local(series, block_pick, tile_pairs, tile_counts):
    picks = block_pick[0, 0]
    rows = rows_to_send(picks, series)
    rows, tile_counts, tile_pairs = lax.optimization_barrier((rows, tile_counts, tile_pairs))
    received = lax.all_to_all(rows, "tile", split_axis=0, concat_axis=0, tiled=True)
    partial_value = tiles(tile_counts, tile_pairs[0, 0], received)
    returned = lax.all_to_all(partial_value, "tile", split_axis=0, concat_axis=0, tiled=True)
    return least_over_bands(owned(picks, returned)).reshape(BLK_DEV * BLOCK)


def solution(mesh):
    in_specs = (
        P("tile"),
        P("band", "tile", None),
        P("band", "tile", None, None),
        P("band", "tile"),
    )
    out_specs = P("tile")
    return jax.shard_map(local, mesh=mesh, in_specs=in_specs, out_specs=out_specs, check_vma=False)
```

```python
import functools

import jax
import jax.numpy as jnp
from jax import lax
from jax.experimental import pallas as pl
from jax.experimental.pallas import tpu as pltpu
from jax.sharding import PartitionSpec as P

SUBLEN = 64
BLOCK = 2048
BLK_DEV = 8
EXCL = 16
LANES = 128
ROW = BLOCK + LANES
ROW_TILES = ROW // LANES
CHUNK = 256
LEAD = 3
LEAST = -1.0 * SUBLEN


def rows_kernel(picks_ref, series_ref, out_ref, extra_ref):
    lane = lax.broadcasted_iota(jnp.int32, (1, LANES), 1)
    body = BLOCK // LANES
    first = lax.axis_index("tile") * BLK_DEV
    head = pltpu.roll(series_ref[0, 0:1], SUBLEN, 1)
    for which in range(BLK_DEV):
        after = series_ref[(which + 1) % BLK_DEV, 0:1]
        extra = jnp.where(lane < SUBLEN, after, head)
        number = (first + which).astype(jnp.float32)
        extra_ref[which : which + 1] = jnp.where(lane == LANES - 1, number, extra)
    for t in range(picks_ref.shape[0]):
        which = picks_ref[t]
        out_ref[t * ROW_TILES : t * ROW_TILES + body] = series_ref[which]
        out_ref[t * ROW_TILES + body : (t + 1) * ROW_TILES] = extra_ref[pl.ds(which, 1)]


def rows_to_send(picks, series):
    owners = picks.shape[0]
    rows = pl.pallas_call(
        rows_kernel,
        out_shape=jax.ShapeDtypeStruct((owners * ROW_TILES, LANES), jnp.float32),
        in_specs=[
            pl.BlockSpec(memory_space=pltpu.SMEM),
            pl.BlockSpec(memory_space=pltpu.VMEM),
        ],
        out_specs=pl.BlockSpec(memory_space=pltpu.VMEM),
        scratch_shapes=[pltpu.VMEM((BLK_DEV, LANES), jnp.float32)],
    )(picks, series.reshape(BLK_DEV, BLOCK // LANES, LANES))
    return rows.reshape(owners, 1, ROW)


def stage_row(recv_ref, owner, wide_ref):
    last = recv_ref.shape[0] - 1
    row = recv_ref[owner]
    extra = row[:, BLOCK:]
    number = jnp.broadcast_to(extra[:, LANES - 1 :], (1, LANES)).astype(jnp.int32)
    following = recv_ref[jnp.minimum(owner + 1, last)][:, BLOCK:]
    following = pltpu.roll(following, SUBLEN, 1)
    following = jnp.where(owner == last, 0.0, following)
    extra = jnp.where((number & (BLK_DEV - 1)) == BLK_DEV - 1, following, extra)
    wide = jnp.broadcast_to(jnp.concatenate([row[:, :BLOCK], extra], axis=1), (8, ROW))
    sub = lax.broadcasted_iota(jnp.int32, (8, ROW), 0)
    for bit in (1, 2, 4):
        wide = jnp.where((sub & bit) != 0, pltpu.roll(wide, ROW - bit, 1), wide)
    wide_ref[...] = wide
    return number


def window_chunk(wide_ref, n):
    size = CHUNK + LANES
    wide = wide_ref[:, n * CHUNK : n * CHUNK + size]
    parts = [wide[:, :CHUNK]]
    for a in range(1, SUBLEN // 8):
        parts.append(pltpu.roll(wide, size - 8 * a, 1)[:, :CHUNK])
    mean = jnp.sum(functools.reduce(jnp.add, parts), axis=0, keepdims=True) * (1.0 / SUBLEN)
    parts = [part - mean for part in parts]
    squares = functools.reduce(jnp.add, [part * part for part in parts])
    spread = jnp.sum(squares, axis=0, keepdims=True) * (1.0 / SUBLEN)
    inverse = lax.rsqrt(spread + 1e-05)
    znorm = jnp.concatenate([part * inverse for part in parts], axis=0)
    high = znorm.astype(jnp.bfloat16)
    low = (znorm - high.astype(jnp.float32)).astype(jnp.bfloat16)
    return high, low


def build_cols(wide_cols, rhs, n):
    here = slice(n * CHUNK, (n + 1) * CHUNK)
    high, low = window_chunk(wide_cols, n)
    rhs[0:64, here] = high
    rhs[64:128, here] = low


def build_rows(wide_rows, lhs, n):
    high, low = window_chunk(wide_rows, n)
    both = jnp.concatenate([high, low], axis=0)
    for q in range(CHUNK // LANES):
        part = both[:, q * LANES : (q + 1) * LANES].T
        at = slice(n * CHUNK + q * LANES, n * CHUNK + (q + 1) * LANES)
        lhs[at, 0:128] = part
        lhs[at, 128:256] = part


def excluded(products, a, b, ahead_ref):
    def masked(part, first_row, offset, ahead):
        gap = (
            offset + first_row
            + lax.broadcasted_iota(jnp.int32, part.shape, 0)
            - lax.broadcasted_iota(jnp.int32, part.shape, 1)
        )
        hit = jnp.logical_and(jnp.abs(gap) < EXCL, ahead_ref[0:1] == ahead)
        return jnp.where(hit, LEAST, part)

    if a == b:
        return masked(products, 0, 0, 0)
    last = BLOCK // LANES - 1
    if a - b in (1, -last):
        ahead = 0 if a - b == 1 else 1
        return jnp.concatenate([masked(products[:EXCL], 0, LANES, ahead), products[EXCL:]], axis=0)
    if a - b in (-1, last):
        ahead = 0 if a - b == -1 else -1
        top = LANES - EXCL
        return jnp.concatenate([products[:top], masked(products[top:], top, -LANES, ahead)], axis=0)
    return products


def multiply_chunk(lhs, rhs, wide_cols, ahead_ref, row_acc, n):
    here = slice(n * CHUNK, (n + 1) * CHUNK)
    high, low = rhs[0:64, here], rhs[64:128, here]
    weights = jnp.concatenate([high, high, low, low], axis=0)
    halves = CHUNK // LANES
    best = [None] * halves
    products = jnp.dot(lhs[...], weights, preferred_element_type=jnp.float32)
    for a in range(BLOCK // LANES):
        at = slice(a * LANES, (a + 1) * LANES)
        strip = None
        for v in range(halves):
            b = n * halves + v
            block = excluded(products[at, v * LANES : (v + 1) * LANES], a, b, ahead_ref)
            strip = block if strip is None else jnp.maximum(strip, block)
            top = jnp.max(block.reshape(LANES // 8, 8, LANES), axis=0)
            best[v] = top if best[v] is None else jnp.maximum(best[v], top)
        row_acc[at] = strip if n == 0 else jnp.maximum(row_acc[at], strip)
    return best


def least_distance(most):
    return 2.0 - most * (2.0 / SUBLEN)


def finish_cols(out_ref, second, best, n):
    for v, top in enumerate(best):
        q = n * (CHUNK // LANES) + v
        least = least_distance(jnp.max(top, axis=0, keepdims=True))
        out_ref[second, q : q + 1] = jnp.minimum(out_ref[second, q : q + 1], least)


def finish_rows(out_ref, first, row_acc, n):
    for q in range(n * CHUNK // LANES, (n + 1) * CHUNK // LANES):
        most = jnp.max(row_acc[q * LANES : (q + 1) * LANES].T, axis=0, keepdims=True)
        out_ref[first, q : q + 1] = jnp.minimum(out_ref[first, q : q + 1], least_distance(most))


def tiles_kernel(count_ref, pairs_ref, recv_ref, out_ref, wide_rows, *buffers):
    sets = (buffers[:5], buffers[5:])
    count = count_ref[0, 0]
    chunks = BLOCK // CHUNK
    out_ref[...] = jnp.full(out_ref.shape, 4.0, jnp.float32)
    sets[1][4][...] = jnp.full(sets[1][4].shape, LEAST, jnp.float32)

    def stage(s, into):
        rows = stage_row(recv_ref, pairs_ref[0, s], wide_rows)
        cols = stage_row(recv_ref, pairs_ref[1, s], into[2])
        into[3][...] = jnp.broadcast_to(rows - cols, into[3].shape)

    stage(0, sets[0])
    for n in range(chunks):
        build_rows(wide_rows, sets[0][0], n)
    for n in range(LEAD):
        build_cols(sets[0][2], sets[0][1], n)

    def phase(now, other, s):
        before = jnp.clip(s - 1, 0, count - 1)
        second = pairs_ref[1, jnp.minimum(s, count - 1)]
        stage(jnp.minimum(s + 1, count - 1), other)
        for n in range(chunks):
            best = multiply_chunk(*now, n)
            ahead = now if n + LEAD < chunks else other
            build_cols(ahead[2], ahead[1], (n + LEAD) % chunks)
            build_rows(wide_rows, other[0], n)
            finish_rows(out_ref, pairs_ref[0, before], other[4], n)
            finish_cols(out_ref, second, best, n)

    def two(i, carry):
        phase(sets[0], sets[1], 2 * i)
        phase(sets[1], sets[0], 2 * i + 1)
        return carry

    lax.fori_loop(0, (count + 1) // 2, two, 0)
    for n in range(chunks):
        finish_rows(out_ref, pairs_ref[0, count - 1], sets[1][4], n)


def tiles(count, pairs, received):
    owners = received.shape[0]
    one = [
        pltpu.VMEM((BLOCK, 256), jnp.bfloat16),
        pltpu.VMEM((2 * SUBLEN, BLOCK), jnp.bfloat16),
        pltpu.VMEM((8, ROW), jnp.float32),
        pltpu.VMEM((8, LANES), jnp.int32),
        pltpu.VMEM((BLOCK, LANES), jnp.float32),
    ]
    return pl.pallas_call(
        tiles_kernel,
        out_shape=jax.ShapeDtypeStruct((owners, BLOCK // LANES, LANES), jnp.float32),
        in_specs=[
            pl.BlockSpec(memory_space=pltpu.SMEM),
            pl.BlockSpec(memory_space=pltpu.SMEM),
            pl.BlockSpec(memory_space=pltpu.VMEM),
        ],
        out_specs=pl.BlockSpec(memory_space=pltpu.VMEM),
        scratch_shapes=[pltpu.VMEM((8, ROW), jnp.float32)] + one * 2,
        compiler_params=pltpu.CompilerParams(vmem_limit_bytes=40 * 1024 * 1024),
    )(count, pairs, received)


def owned_kernel(picks_ref, returned_ref, out_ref):
    out_ref[...] = jnp.full(out_ref.shape, 4.0, jnp.float32)
    for t in range(returned_ref.shape[0]):
        which = picks_ref[t]
        out_ref[which] = jnp.minimum(out_ref[which], returned_ref[t])


def owned(picks, returned):
    return pl.pallas_call(
        owned_kernel,
        out_shape=pltpu.VMEM((BLK_DEV,) + returned.shape[1:], jnp.float32),
        in_specs=[
            pl.BlockSpec(memory_space=pltpu.SMEM),
            pl.BlockSpec(memory_space=pltpu.VMEM),
        ],
        out_specs=pl.BlockSpec(memory_space=pltpu.VMEM),
    )(
        pltpu.with_memory_space_constraint(picks, pltpu.VMEM),
        pltpu.with_memory_space_constraint(returned, pltpu.VMEM),
    )


def least_over_bands(mine):
    bands = lax.axis_size("band")
    others = [
        lax.ppermute(mine, "band", [(i, (i + step) % bands) for i in range(bands)])
        for step in range(1, bands)
    ]
    return functools.reduce(jnp.minimum, others, mine)


def local(series, block_pick, tile_pairs, tile_counts):
    picks = block_pick[0, 0]
    rows = rows_to_send(picks, series)
    rows, tile_counts, tile_pairs = lax.optimization_barrier((rows, tile_counts, tile_pairs))
    received = lax.all_to_all(rows, "tile", split_axis=0, concat_axis=0, tiled=True)
    partial_value = tiles(tile_counts, tile_pairs[0, 0], received)
    returned = lax.all_to_all(partial_value, "tile", split_axis=0, concat_axis=0, tiled=True)
    return least_over_bands(owned(picks, returned)).reshape(BLK_DEV * BLOCK)


def solution(mesh):
    in_specs = (
        P("tile"),
        P("band", "tile", None),
        P("band", "tile", None, None),
        P("band", "tile"),
    )
    out_specs = P("tile")
    return jax.shard_map(local, mesh=mesh, in_specs=in_specs, out_specs=out_specs, check_vma=False)
```
